32 devices in a mesh: gx: 8 (over y, x, core), gz: 4 (over z).
Axes of the slice: x: 2, y: 2, z: 4, core: 2. Of those that a mesh axis runs over, the one named last changes fastest.
Arguments:
- heat_adjoint: float32 [128, 64, 512], P('gx', None, 'gz'), may hold values from -6 to 6
- moisture_adjoint: float32 [128, 64, 512], P('gx', None, 'gz'), may hold values from -6 to 6
- conductivity: float32 [128, 64, 512], P('gx', None, 'gz'), may hold values from 0.02 to 0.12
- labels: int32 [128, 64, 512], P('gx', None, 'gz'), may hold values from 0 to 3
- moisture_rate: float32 [4], replicated, may hold values from 0.02 to 0.1
- exchange_rates: float32 [2, 4], replicated, may hold values from 0.02 to 0.1
- checkpoints: float32 [4, 128, 64, 512], P(None, 'gx', None, 'gz'), may hold values from -6 to 6
- slot_of_step: int32 [4], replicated, may hold values from 0 to 3, each once
Outputs:
- heat_out: float32 [128, 64, 512], P('gx', None, 'gz')
- moisture_out: float32 [128, 64, 512], P('gx', None, 'gz')
- smoothed_gradient: float32 [64, 32, 256], P(None, 'gx', 'gz')
The draws below stay inside these ranges and needn't reach their ends.
Inputs may be any that keep to these rules, and one draw needn't show every extreme that they name: slot_of_step names every slot once.
All inputs are finite; a program needn't handle non-finite values.
Results may differ from the reference program's by a relative error of at most 0.00014.
Values sent between devices are 32-bit elements; how exact they have to be, the bound alone decides.
A program may use at most 128 MiB of HBM per device.

```python
import math
import jax
import jax.numpy as jnp
from jax import lax

NY = 64
STEPS = 4
NX = 128
NZ = 512
NXC = 64
NYC = 32
NZC = 256


def with_ends(values, key, smallest, largest):
    index_at = [jax.random.randint(jax.random.fold_in(key, axis), (), 0, length) for axis, length in enumerate(values.shape)]
    widest = values.shape.index(max(values.shape))
    next_to = index_at[:widest] + [(index_at[widest] + 1) % values.shape[widest]] + index_at[widest + 1:]
    return values.at[tuple(index_at)].set(smallest).at[tuple(next_to)].set(largest)


def block_scale(key, extent, pieces, low, high):
    def one(axis_at, shards_of):
        heights = jax.random.uniform(jax.random.fold_in(jax.random.fold_in(key, 6), axis_at), (shards_of,), jnp.float32, low / len(pieces), high / len(pieces))
        return jnp.repeat(jnp.exp(heights), extent[axis_at] // shards_of).reshape((-1,) + (1,) * (len(extent) - axis_at - 1))

    factor_of = one(*pieces[0])
    for cut in pieces[1:]:
        factor_of = factor_of * one(*cut)
    return factor_of


def scatter_about(key, extent, width, limit, split=(), held_as=jnp.bfloat16):
    array = width * jax.random.normal(key, extent, jnp.float32)
    if split:
        array = array * block_scale(key, extent, split, -0.22, 0.18)
    return jnp.clip(array, -limit, limit).astype(held_as)


def setup_inputs(seed: int = 0) -> dict:
    key_of = jax.random.split(jax.random.key(seed), 9)
    return {
        "heat_adjoint": scatter_about(key_of[0], (NX, NY, NZ), 1.0, 6.0, ((0, 8), (2, 4)), jnp.float32),
        "moisture_adjoint": scatter_about(key_of[1], (NX, NY, NZ), 1.0, 6.0, ((0, 8), (2, 4)), jnp.float32),
        "conductivity": jnp.clip(jnp.exp(math.log(0.12) - 1.7917595 * jax.random.uniform(key_of[2], (NX, NY, NZ), jnp.float32) ** block_scale(key_of[2], (NX, NY, NZ), ((0, 8), (2, 4)), -0.2, 0.2)), 0.02, 0.12),
        "labels": with_ends(jax.random.randint(key_of[3], (NX, NY, NZ), 0, 4), jax.random.fold_in(key_of[3], 1), 0, 3).astype(jnp.int32),
        "moisture_rate": jnp.clip(jax.random.uniform(key_of[4], (4,), jnp.float32, 0.02, 0.1), 0.02, 0.1),
        "exchange_rates": jnp.clip(jax.random.uniform(key_of[5], (2, 4), jnp.float32, 0.02, 0.1), 0.02, 0.1),
        "checkpoints": scatter_about(key_of[6], (STEPS, NX, NY, NZ), 1.0, 6.0, ((1, 8), (3, 4)), jnp.float32),
        "slot_of_step": jax.random.permutation(key_of[7], STEPS).astype(jnp.int32),
    }


PRIOR_WEIGHT = 200.0
NEIGHBOURS = ((2, 1), (0, 1), (1, 2), (1, 0))

def window(values, along_first, along_last):
    return values[along_first:values.shape[0] - 2 + along_first, :, along_last:values.shape[2] - 2 + along_last]

def laplace(values, coeffs, inside):
    centre = window(values, 1, 1)
    coef_centre = window(coeffs, 1, 1)
    in_centre = window(inside, 1, 1)
    summed = jnp.zeros_like(centre)
    for along_first, along_last in NEIGHBOURS:
        weight = 0.5 * (coef_centre + window(coeffs, along_first, along_last)) * in_centre * window(inside, along_first, along_last)
        summed = summed + weight * (window(values, along_first, along_last) - centre)
    flux_along = 0.5 * (coef_centre[:, 1:] + coef_centre[:, :-1]) * (centre[:, 1:] - centre[:, :-1])
    return summed + jnp.pad(flux_along, ((0, 0), (0, 1), (0, 0))) - jnp.pad(flux_along, ((0, 0), (1, 0), (0, 0)))

def sensitivity(snapshot, adjoint, inside):
    centre_u = window(snapshot, 1, 1)
    centre_l = window(adjoint, 1, 1)
    in_centre = window(inside, 1, 1)
    summed = jnp.zeros_like(centre_u)
    for along_first, along_last in NEIGHBOURS:
        summed = summed + in_centre * window(inside, along_first, along_last) * (window(snapshot, along_first, along_last) - centre_u) * (window(adjoint, along_first, along_last) - centre_l)
    product_along = (centre_u[:, 1:] - centre_u[:, :-1]) * (centre_l[:, 1:] - centre_l[:, :-1])
    summed = summed + jnp.pad(product_along, ((0, 0), (0, 1), (0, 0))) + jnp.pad(product_along, ((0, 0), (1, 0), (0, 0)))
    return -0.5 * summed

def advance(heat_ext, moist_ext, coeffs_stack, inside):
    heat_centre = window(heat_ext, 1, 1)
    moist_centre = window(moist_ext, 1, 1)
    rate_a = window(coeffs_stack[2], 1, 1)
    rate_b = window(coeffs_stack[3], 1, 1)
    new_heat = heat_centre + laplace(heat_ext, coeffs_stack[0], inside) - rate_a * heat_centre + rate_b * moist_centre
    new_moist = moist_centre + laplace(moist_ext, coeffs_stack[1], inside) + rate_a * heat_centre - rate_b * moist_centre
    return (new_heat, new_moist)

def smooth_columns(coarse):
    length = coarse.shape[0]
    columns = coarse.reshape(length, -1)
    position = jnp.arange(length)
    lower = jnp.where(position == 0, 0.0, -PRIOR_WEIGHT).astype(columns.dtype)
    upper = jnp.where(position == length - 1, 0.0, -PRIOR_WEIGHT).astype(columns.dtype)
    ends = (position == 0) | (position == length - 1)
    middle = jnp.where(ends, 1.0 + PRIOR_WEIGHT, 1.0 + 2.0 * PRIOR_WEIGHT).astype(columns.dtype)
    return lax.linalg.tridiagonal_solve(lower, middle, upper, columns).reshape(coarse.shape)

def pad_grid(values):
    return jnp.pad(values, ((1, 1), (0, 0), (1, 1)))

def reference(heat_adjoint, moisture_adjoint, conductivity, labels, moisture_rate, exchange_rates, checkpoints, slot_of_step):
    rate_m = moisture_rate[labels]
    rate_a = exchange_rates[0][labels]
    rate_b = exchange_rates[1][labels]
    coeffs_stack = jnp.stack([pad_grid(conductivity), pad_grid(rate_m), pad_grid(rate_a), pad_grid(rate_b)])
    inside = pad_grid(jnp.ones((NX, 1, NZ), dtype=conductivity.dtype))
    heat_now = heat_adjoint
    moist_now = moisture_adjoint
    gradient = jnp.zeros_like(heat_adjoint)
    for step_num in range(STEPS):
        snapshot = lax.dynamic_index_in_dim(checkpoints, slot_of_step[step_num], 0, keepdims=False)
        heat_ext = pad_grid(heat_now)
        gradient = gradient + sensitivity(pad_grid(snapshot), heat_ext, inside)
        heat_now, moist_now = advance(heat_ext, pad_grid(moist_now), coeffs_stack, inside)
    masked = jnp.where(labels == 0, gradient, jnp.zeros_like(gradient))
    coarse = masked.reshape(NXC, 2, NYC, 2, NZC, 2).sum(axis=(1, 3, 5))
    return (heat_now, moist_now, smooth_columns(coarse))
```

```python
import functools

import jax
import jax.numpy as jnp
import numpy as np
from jax import lax
from jax.experimental import pallas as pl
from jax.experimental.pallas import tpu as pltpu
from jax.sharding import PartitionSpec as P

PRIOR_WEIGHT = 200.0
MESH = pl.DeviceIdType.MESH


def smoother(length):
    d = np.zeros((length, length))
    for i in range(length - 1):
        d[i, i] += 1.0
        d[i + 1, i + 1] += 1.0
        d[i, i + 1] -= 1.0
        d[i + 1, i] -= 1.0
    return np.linalg.inv(np.eye(length) + PRIOR_WEIGHT * d).astype(np.float32)


class Swap:
    def __init__(self, here, count, target, sems, index, low_face, high_face, low_halo, high_halo):
        send_sem, recv_sem = sems
        self.here, self.count = here, count
        self.faces = (low_face, high_face)
        self.halos = (low_halo, high_halo)
        self.down = pltpu.make_async_remote_copy(
            src_ref=low_face, dst_ref=high_halo,
            send_sem=send_sem.at[2 * index], recv_sem=recv_sem.at[2 * index],
            device_id=target(lax.rem(here + count - 1, count)), device_id_type=MESH)
        self.up = pltpu.make_async_remote_copy(
            src_ref=high_face, dst_ref=low_halo,
            send_sem=send_sem.at[2 * index + 1], recv_sem=recv_sem.at[2 * index + 1],
            device_id=target(lax.rem(here + 1, count)), device_id_type=MESH)

    def start(self):
        pl.when(self.here > 0)(self.down.start)
        pl.when(self.here < self.count - 1)(self.up.start)

    def recv(self):
        pl.when(self.here < self.count - 1)(self.down.wait_recv)
        pl.when(self.here > 0)(self.up.wait_recv)

    def sent(self):
        pl.when(self.here > 0)(self.down.wait_send)
        pl.when(self.here < self.count - 1)(self.up.wait_send)


def kernel(
    n_x, n_z, steps,
    heat, moist, cond, labels, rate_t, exch_t, checks, slots, minv,
    out_h, out_m, out_s,
    hm, cf, ck, lab, ra, rb, wx, wy, wzp, wzm,
    zsend_lo, zsend_hi, zlo, zhi, zcsend_lo, zcsend_hi, zclo, zchi,
    grad, hm_out, csend, crecv,
    local_sem, send_sem, recv_sem, c_send_sem, c_recv_sem,
):
    nx, ny, nz = lab.shape
    rows = ny // n_x
    gx, gz = lax.axis_index("gx"), lax.axis_index("gz")
    sems = (send_sem, recv_sem)
    to_x = lambda i: (i, gz)
    to_z = lambda i: (gx, i)
    inner = pl.ds(1, nx)

    locals_ = [
        pltpu.make_async_copy(labels, lab, local_sem.at[0]),
        pltpu.make_async_copy(heat, hm.at[0, 0, inner], local_sem.at[1]),
        pltpu.make_async_copy(moist, hm.at[0, 1, inner], local_sem.at[2]),
        pltpu.make_async_copy(cond, cf.at[0, inner], local_sem.at[3]),
        pltpu.make_async_copy(checks, ck.at[:, inner], local_sem.at[4]),
    ]
    for copy in locals_:
        copy.start()

    barrier = pltpu.get_barrier_semaphore()
    for d in range(1, n_x):
        pl.semaphore_signal(barrier, inc=1, device_id=(lax.rem(gx + d, n_x), gz), device_id_type=MESH)

    @pl.when(gz > 0)
    def _():
        pl.semaphore_signal(barrier, inc=1, device_id=(gx, gz - 1), device_id_type=MESH)

    @pl.when(gz < n_z - 1)
    def _():
        pl.semaphore_signal(barrier, inc=1, device_id=(gx, gz + 1), device_id_type=MESH)

    beside = jnp.where(gz > 0, 1, 0) + jnp.where(gz < n_z - 1, 1, 0)
    pl.semaphore_wait(barrier, n_x - 1 + beside)

    def x_swap(index, low_face, high_face, low_halo, high_halo):
        return Swap(gx, n_x, to_x, sems, index, low_face, high_face, low_halo, high_halo)

    def z_swap(index, low_face, high_face, low_halo, high_halo):
        return Swap(gz, n_z, to_z, sems, index, low_face, high_face, low_halo, high_halo)

    last = nx - 1
    x_first = [
        x_swap(0, heat.at[0], heat.at[last], hm.at[0, 0, 0], hm.at[0, 0, nx + 1]),
        x_swap(1, moist.at[0], moist.at[last], hm.at[0, 1, 0], hm.at[0, 1, nx + 1]),
        x_swap(2, cond.at[0], cond.at[last], cf.at[0, 0], cf.at[0, nx + 1]),
        x_swap(3, cf.at[1, 1], cf.at[1, nx], cf.at[1, 0], cf.at[1, nx + 1]),
    ]
    x_check = x_swap(4, checks.at[:, 0], checks.at[:, last], ck.at[:, 0], ck.at[:, nx + 1])
    z_check = z_swap(5, zcsend_lo, zcsend_hi, zclo, zchi)
    x_step = [None] + [
        x_swap(5 + t, hm.at[t, :, 1], hm.at[t, :, nx], hm.at[t, :, 0], hm.at[t, :, nx + 1])
        for t in range(1, steps)
    ]
    z_step = [
        z_swap(5 + steps + t, zsend_lo.at[t], zsend_hi.at[t], zlo.at[t], zhi.at[t])
        for t in range(steps)
    ]

    for swap in x_first[:3]:
        swap.start()

    lane = lax.broadcasted_iota(jnp.int32, (ny, nz), 1)
    row = lax.broadcasted_iota(jnp.int32, (ny, nz), 0)
    at_first, at_last = lane == 0, lane == nz - 1
    no_up = row == ny - 1

    def pick(label, table):
        return jnp.where(label == 0, table[0], jnp.where(label == 1, table[1], jnp.where(label == 2, table[2], table[3])))

    locals_[0].wait()
    table_m = [rate_t[i] for i in range(4)]
    table_a = [exch_t[0, i] for i in range(4)]
    table_b = [exch_t[1, i] for i in range(4)]

    def rates(x, carry):
        label = lab[x]
        cf[1, x + 1] = pick(label, table_m)
        ra[x] = pick(label, table_a)
        rb[x] = pick(label, table_b)
        return carry

    lax.fori_loop(0, nx, rates, 0)
    x_first[3].start()
    x_check.start()

    def pack(planes, lo_ref, hi_ref):
        def body(x, carry):
            lo, hi = carry
            for i, read in enumerate(planes):
                k = i * nx + x
                v = read(x)
                mine = lane == k
                lo = jnp.where(mine, pltpu.roll(v, k, 1), lo)
                hi = jnp.where(mine, pltpu.roll(v, k + 1, 1), hi)
            return lo, hi

        zero = jnp.zeros((ny, nz), jnp.float32)
        lo, hi = lax.fori_loop(0, nx, body, (zero, zero))
        lo_ref[...] = lo
        hi_ref[...] = hi

    for copy in locals_[1:4]:
        copy.wait()
    pack(
        [lambda x: hm[0, 0, x + 1], lambda x: hm[0, 1, x + 1], lambda x: cf[0, x + 1], lambda x: cf[1, x + 1]],
        zsend_lo.at[0], zsend_hi.at[0],
    )
    z_step[0].start()
    locals_[4].wait()
    for s in range(steps):
        pack([lambda x, s=s: ck[s, x + 1]], zcsend_lo.at[s], zcsend_hi.at[s])
    z_check.start()

    def fill(swap):
        @pl.when(swap.here == 0)
        def _():
            swap.halos[0][...] = swap.faces[0][...]

        @pl.when(swap.here == swap.count - 1)
        def _():
            swap.halos[1][...] = swap.faces[1][...]

    def fill_x(here_lo, here_hi):
        @pl.when(gx == 0)
        def _():
            here_lo[0][...] = here_lo[1][...]

        @pl.when(gx == n_x - 1)
        def _():
            here_hi[0][...] = here_hi[1][...]

    def z_low(ref, k):
        return pltpu.roll(ref, lax.rem(nz - k, nz), 1)

    def z_high(ref, k):
        return pltpu.roll(ref, nz - 1 - k, 1)

    def along_z(v, low_pack, high_pack, k):
        up = jnp.where(at_last, z_high(high_pack, k), pltpu.roll(v, nz - 1, 1))
        down = jnp.where(at_first, z_low(low_pack, k), pltpu.roll(v, 1, 1))
        return up, down

    def advance_plane(t, x):
        news = []
        olds = []
        for f in range(2):
            v = hm[t, f, x + 1]
            up, down = along_z(v, zlo[t], zhi[t], f * nx + x)
            flux = wy[f, x] * (pltpu.roll(v, ny - 1, 0) - v)
            total = (
                wx[f, x + 1] * (hm[t, f, x + 2] - v)
                + wx[f, x] * (hm[t, f, x] - v)
                + (flux - pltpu.roll(flux, 1, 0))
                + wzp[f, x] * (up - v)
                + wzm[f, x] * (down - v)
            )
            olds.append(v)
            news.append(v + total)
        trade = ra[x] * olds[0] - rb[x] * olds[1]
        return news[0] - trade, news[1] + trade

    def sense_plane(t, slot, x):
        u = ck[slot, x + 1]
        v = hm[t, 0, x + 1]
        u_up, u_down = along_z(u, zclo[slot], zchi[slot], x)
        v_up, v_down = along_z(v, zlo[t], zhi[t], x)
        across = (pltpu.roll(u, ny - 1, 0) - u) * (pltpu.roll(v, ny - 1, 0) - v)
        across = jnp.where(no_up, 0.0, across)
        return (
            (ck[slot, x + 2] - u) * (hm[t, 0, x + 2] - v)
            + (ck[slot, x] - u) * (hm[t, 0, x] - v)
            + (across + pltpu.roll(across, 1, 0))
            + (u_up - u) * (v_up - v)
            + (u_down - u) * (v_down - v)
        )

    for swap in x_first:
        swap.recv()
    z_step[0].recv()
    fill(z_step[0])
    for f in range(2):
        fill_x((hm.at[0, f, 0], hm.at[0, f, 1]), (hm.at[0, f, nx + 1], hm.at[0, f, nx]))
        fill_x((cf.at[f, 0], cf.at[f, 1]), (cf.at[f, nx + 1], cf.at[f, nx]))

    def weights(x, carry):
        for f in range(2):
            c = cf[f, x + 1]
            up, down = along_z(c, zlo[0], zhi[0], (2 + f) * nx + x)
            wx[f, x + 1] = 0.5 * (c + cf[f, x + 2])
            wy[f, x] = jnp.where(no_up, 0.0, 0.5 * (c + pltpu.roll(c, ny - 1, 0)))
            wzp[f, x] = 0.5 * (c + up)
            wzm[f, x] = 0.5 * (c + down)
        return carry

    for f in range(2):
        wx[f, 0] = 0.5 * (cf[f, 0] + cf[f, 1])
    lax.fori_loop(0, nx, weights, 0)

    for t in range(steps):
        slot = slots[t]
        if t > 0:
            x_step[t].recv()
            z_step[t].recv()
            fill(x_step[t])
            fill(z_step[t])
        if t < steps - 1:
            def put(x, carry, t=t):
                h, m = advance_plane(t, x)
                hm[t + 1, 0, x + 1] = h
                hm[t + 1, 1, x + 1] = m
                return carry

            put(0, 0)
            put(last, 0)
            x_step[t + 1].start()
            lax.fori_loop(1, last, put, 0)
            pack(
                [lambda x, t=t: hm[t + 1, 0, x + 1], lambda x, t=t: hm[t + 1, 1, x + 1]],
                zsend_lo.at[t + 1], zsend_hi.at[t + 1],
            )
            z_step[t + 1].start()
        if t == 0:
            x_check.recv()
            z_check.recv()
            fill(z_check)
            fill_x((ck.at[:, 0], ck.at[:, 1]), (ck.at[:, nx + 1], ck.at[:, nx]))
        if t < steps - 1:
            def sense(x, carry, t=t, slot=slot):
                g = sense_plane(t, slot, x)
                grad[x] = g if t == 0 else grad[x] + g
                return carry

            lax.fori_loop(0, nx, sense, 0)
        else:
            def coarsen(i, carry, t=t, slot=slot):
                total = jnp.zeros((ny, nz), jnp.float32)
                for j in range(2):
                    x = 2 * i + j
                    g = -0.5 * (grad[x] + sense_plane(t, slot, x))
                    total = total + jnp.where(lab[x] == 0, g, 0.0)
                for p in range(n_x):
                    csend[p, i] = total[p * rows : (p + 1) * rows]
                return carry

            lax.fori_loop(0, nx // 2, coarsen, 0)

    spread = []
    for d in range(1, n_x):
        peer = lax.rem(gx + d, n_x)
        copy = pltpu.make_async_remote_copy(
            src_ref=csend.at[peer], dst_ref=crecv.at[gx],
            send_sem=c_send_sem.at[d], recv_sem=c_recv_sem.at[d],
            device_id=(peer, gz), device_id_type=MESH)
        copy.start()
        spread.append(copy)
    crecv[gx] = csend[gx]

    def finish(x, carry):
        h, m = advance_plane(steps - 1, x)
        hm_out[0, x] = h
        hm_out[1, x] = m
        return carry

    lax.fori_loop(0, nx, finish, 0)
    outs = [
        pltpu.make_async_copy(hm_out.at[0], out_h, local_sem.at[5]),
        pltpu.make_async_copy(hm_out.at[1], out_m, local_sem.at[6]),
    ]
    for copy in outs:
        copy.start()

    for copy in spread:
        copy.wait_recv()
    length = n_x * (nx // 2)
    pair_row = lax.broadcasted_iota(jnp.int32, (nz, nz // 2), 0)
    pair_col = lax.broadcasted_iota(jnp.int32, (nz, nz // 2), 1)
    first = 2 * pair_col
    pairs = jnp.where((pair_row == first) | (pair_row == first + 1), 1.0, 0.0)
    for k in range(rows // 2):
        columns = (crecv[:, :, 2 * k, :] + crecv[:, :, 2 * k + 1, :]).reshape(length, nz)
        solved = jnp.dot(minv[...], columns, precision=lax.Precision.HIGHEST, preferred_element_type=jnp.float32)
        out_s[:, k, :] = jnp.dot(solved, pairs, precision=lax.Precision.HIGHEST, preferred_element_type=jnp.float32)

    for copy in spread:
        copy.wait_send()
    for swap in x_first + [x_check, z_check] + x_step[1:] + z_step:
        swap.sent()
    for copy in outs:
        copy.wait()


def on_device(n_x, n_z, heat, moist, cond, labels, rates, exchange, checks, slots):
    nx, ny, nz = heat.shape
    steps = checks.shape[0]
    half = nx // 2
    length = n_x * half
    rows = ny // n_x
    f32 = jnp.float32
    hbm = pl.BlockSpec(memory_space=pl.ANY)
    smem = pl.BlockSpec(memory_space=pltpu.SMEM)
    vmem = pl.BlockSpec(memory_space=pltpu.VMEM)
    n_swaps = 7 + 2 * steps
    scratch = [
        pltpu.VMEM((steps, 2, nx + 2, ny, nz), f32),
        pltpu.VMEM((2, nx + 2, ny, nz), f32),
        pltpu.VMEM((steps, nx + 2, ny, nz), f32),
        pltpu.VMEM((nx, ny, nz), jnp.int32),
        pltpu.VMEM((nx, ny, nz), f32),
        pltpu.VMEM((nx, ny, nz), f32),
        pltpu.VMEM((2, nx + 1, ny, nz), f32),
        pltpu.VMEM((2, nx, ny, nz), f32),
        pltpu.VMEM((2, nx, ny, nz), f32),
        pltpu.VMEM((2, nx, ny, nz), f32),
    ] + [pltpu.VMEM((steps, ny, nz), f32) for _ in range(8)] + [
        pltpu.VMEM((nx, ny, nz), f32),
        pltpu.VMEM((2, nx, ny, nz), f32),
        pltpu.VMEM((n_x, half, rows, nz), f32),
        pltpu.VMEM((n_x, half, rows, nz), f32),
        pltpu.SemaphoreType.DMA((7,)),
        pltpu.SemaphoreType.DMA((2 * n_swaps,)),
        pltpu.SemaphoreType.DMA((2 * n_swaps,)),
        pltpu.SemaphoreType.DMA((n_x,)),
        pltpu.SemaphoreType.DMA((n_x,)),
    ]
    return pl.pallas_call(
        functools.partial(kernel, n_x, n_z, steps),
        out_shape=(
            jax.ShapeDtypeStruct(heat.shape, f32),
            jax.ShapeDtypeStruct(heat.shape, f32),
            jax.ShapeDtypeStruct((length, rows // 2, nz // 2), f32),
        ),
        in_specs=[hbm, hbm, hbm, hbm, smem, smem, hbm, smem, vmem],
        out_specs=(hbm, hbm, vmem),
        scratch_shapes=scratch,
        compiler_params=pltpu.CompilerParams(
            collective_id=0, has_side_effects=True, vmem_limit_bytes=48 * 1024 * 1024
        ),
        name="adjoint_window",
    )(heat, moist, cond, labels, rates, exchange, checks, slots, jnp.asarray(smoother(length)))


def solution(mesh):
    grid = P("gx", None, "gz")
    in_specs = (grid, grid, grid, grid, P(), P(), P(None, "gx", None, "gz"), P())
    out_specs = (grid, grid, P(None, "gx", "gz"))
    return jax.shard_map(
        functools.partial(on_device, mesh.shape["gx"], mesh.shape["gz"]),
        mesh=mesh, in_specs=in_specs, out_specs=out_specs, check_vma=False,
    )
```

```python
import functools

import jax
import jax.numpy as jnp
import numpy as np
from jax import lax
from jax.experimental import pallas as pl
from jax.experimental.pallas import tpu as pltpu
from jax.sharding import PartitionSpec as P

PRIOR_WEIGHT = 200.0
MESH = pl.DeviceIdType.MESH
TOGETHER = 4


def smoother(length):
    d = np.zeros((length, length))
    for i in range(length - 1):
        d[i, i] += 1.0
        d[i + 1, i + 1] += 1.0
        d[i, i + 1] -= 1.0
        d[i + 1, i] -= 1.0
    return np.linalg.inv(np.eye(length) + PRIOR_WEIGHT * d).astype(np.float32)


class Swap:
    def __init__(self, here, count, target, sems, index, low_face, high_face, low_halo, high_halo):
        send_sem, recv_sem = sems
        self.here, self.count = here, count
        self.faces = (low_face, high_face)
        self.halos = (low_halo, high_halo)
        self.down = pltpu.make_async_remote_copy(
            src_ref=low_face, dst_ref=high_halo,
            send_sem=send_sem.at[2 * index], recv_sem=recv_sem.at[2 * index],
            device_id=target(lax.rem(here + count - 1, count)), device_id_type=MESH)
        self.up = pltpu.make_async_remote_copy(
            src_ref=high_face, dst_ref=low_halo,
            send_sem=send_sem.at[2 * index + 1], recv_sem=recv_sem.at[2 * index + 1],
            device_id=target(lax.rem(here + 1, count)), device_id_type=MESH)

    def start(self):
        pl.when(self.here > 0)(self.down.start)
        pl.when(self.here < self.count - 1)(self.up.start)

    def recv(self):
        pl.when(self.here < self.count - 1)(self.down.wait_recv)
        pl.when(self.here > 0)(self.up.wait_recv)

    def sent(self):
        pl.when(self.here > 0)(self.down.wait_send)
        pl.when(self.here < self.count - 1)(self.up.wait_send)


def kernel(
    n_x, n_z, steps,
    heat, moist, cond, labels, rate_t, exch_t, checks, slots, minv,
    out_h, out_m, out_s,
    hm, cf, ck, lab, ra, rb, wx, wy, wzp, wzm,
    zsend, zlo, zhi, zhalo, zcsend, zclo, zchi, zchalo,
    grad, hm_out, csend, crecv,
    local_sem, send_sem, recv_sem, c_send_sem, c_recv_sem,
):
    nx, ny, nz = lab.shape
    rows = ny // n_x
    gx, gz = lax.axis_index("gx"), lax.axis_index("gz")
    sems = (send_sem, recv_sem)

    def over(low, high, body):
        def block(i, carry):
            for j in range(TOGETHER):
                body(low + i * TOGETHER + j)
            return carry

        lax.fori_loop(0, (high - low) // TOGETHER, block, 0)
        for x in range(low + (high - low) // TOGETHER * TOGETHER, high):
            body(x)

    to_x = lambda i: (i, gz)
    to_z = lambda i: (gx, i)
    inner = pl.ds(1, nx)

    locals_ = [
        pltpu.make_async_copy(labels, lab, local_sem.at[0]),
        pltpu.make_async_copy(heat, hm.at[0, 0, inner], local_sem.at[1]),
        pltpu.make_async_copy(moist, hm.at[0, 1, inner], local_sem.at[2]),
        pltpu.make_async_copy(cond, cf.at[0, inner], local_sem.at[3]),
        pltpu.make_async_copy(checks, ck.at[:, inner], local_sem.at[4]),
    ]
    for copy in locals_:
        copy.start()

    barrier = pltpu.get_barrier_semaphore()
    for d in range(1, n_x):
        pl.semaphore_signal(barrier, inc=1, device_id=(lax.rem(gx + d, n_x), gz), device_id_type=MESH)

    @pl.when(gz > 0)
    def _():
        pl.semaphore_signal(barrier, inc=1, device_id=(gx, gz - 1), device_id_type=MESH)

    @pl.when(gz < n_z - 1)
    def _():
        pl.semaphore_signal(barrier, inc=1, device_id=(gx, gz + 1), device_id_type=MESH)

    beside = jnp.where(gz > 0, 1, 0) + jnp.where(gz < n_z - 1, 1, 0)
    pl.semaphore_wait(barrier, n_x - 1 + beside)

    def x_swap(index, low_face, high_face, low_halo, high_halo):
        return Swap(gx, n_x, to_x, sems, index, low_face, high_face, low_halo, high_halo)

    def z_swap(index, low_face, high_face, low_halo, high_halo):
        return Swap(gz, n_z, to_z, sems, index, low_face, high_face, low_halo, high_halo)

    last = nx - 1
    x_first = [
        x_swap(0, heat.at[0], heat.at[last], hm.at[0, 0, 0], hm.at[0, 0, nx + 1]),
        x_swap(1, moist.at[0], moist.at[last], hm.at[0, 1, 0], hm.at[0, 1, nx + 1]),
        x_swap(2, cond.at[0], cond.at[last], cf.at[0, 0], cf.at[0, nx + 1]),
        x_swap(3, cf.at[1, 1], cf.at[1, nx], cf.at[1, 0], cf.at[1, nx + 1]),
    ]
    x_check = x_swap(4, checks.at[:, 0], checks.at[:, last], ck.at[:, 0], ck.at[:, nx + 1])
    z_check = z_swap(5, zcsend, zcsend, zclo, zchi)
    x_step = [None] + [
        x_swap(5 + t, hm.at[t, :, 1], hm.at[t, :, nx], hm.at[t, :, 0], hm.at[t, :, nx + 1])
        for t in range(1, steps)
    ]
    z_step = [
        z_swap(5 + steps + t, zsend.at[t], zsend.at[t], zlo.at[t], zhi.at[t])
        for t in range(steps)
    ]

    for swap in x_first[:3]:
        swap.start()

    lane = lax.broadcasted_iota(jnp.int32, (ny, nz), 1)
    row = lax.broadcasted_iota(jnp.int32, (ny, nz), 0)
    at_first, at_last = lane == 0, lane == nz - 1
    no_up = row == ny - 1
    pair = lax.shift_right_logical(lane, 1)
    even = lax.rem(lane, 2) == 0

    def pick(label, table):
        return jnp.where(label == 0, table[0], jnp.where(label == 1, table[1], jnp.where(label == 2, table[2], table[3])))

    locals_[0].wait()
    table_m = [rate_t[i] for i in range(4)]
    table_a = [exch_t[0, i] for i in range(4)]
    table_b = [exch_t[1, i] for i in range(4)]

    def rates(x):
        label = lab[x]
        cf[1, x + 1] = pick(label, table_m)
        ra[x] = pick(label, table_a)
        rb[x] = pick(label, table_b)

    over(0, nx, rates)
    x_first[3].start()
    x_check.start()

    def pack(planes, ref):
        total = jnp.zeros((ny, nz), jnp.float32)
        for j, v in enumerate(planes):
            total = jnp.where(pair == j, pltpu.roll(v, (2 * j + 1) % nz, 1), total)
        ref[...] = total

    def merge(own, low_pack, high_pack, ref):
        ref[...] = own[...]

        @pl.when(gz > 0)
        def _():
            ref[...] = jnp.where(even, ref[...], pltpu.roll(low_pack[...], 1, 1))

        @pl.when(gz < n_z - 1)
        def _():
            ref[...] = jnp.where(even, pltpu.roll(high_pack[...], nz - 1, 1), ref[...])

    for copy in locals_[1:4]:
        copy.wait()
    pack([src[i, x + 1] for src in (hm.at[0], cf) for i in range(2) for x in range(nx)], zsend.at[0])
    z_step[0].start()
    locals_[4].wait()
    for s in range(steps):
        pack([ck[s, x + 1] for x in range(nx)], zcsend.at[s])
    z_check.start()

    def fill(swap):
        @pl.when(swap.here == 0)
        def _():
            swap.halos[0][...] = swap.faces[0][...]

        @pl.when(swap.here == swap.count - 1)
        def _():
            swap.halos[1][...] = swap.faces[1][...]

    def fill_x(here_lo, here_hi):
        @pl.when(gx == 0)
        def _():
            here_lo[0][...] = here_lo[1][...]

        @pl.when(gx == n_x - 1)
        def _():
            here_hi[0][...] = here_hi[1][...]

    def along_z(v, halo, j):
        ends = pltpu.roll(halo, nz - 1 - 2 * j, 1)
        up = jnp.where(at_last, ends, pltpu.roll(v, nz - 1, 1))
        down = jnp.where(at_first, ends, pltpu.roll(v, 1, 1))
        return up, down

    def advance_plane(t, x):
        news = []
        olds = []
        for f in range(2):
            v = hm[t, f, x + 1]
            up, down = along_z(v, zhalo[t], f * nx + x)
            flux = wy[f, x] * (pltpu.roll(v, ny - 1, 0) - v)
            total = (
                wx[f, x + 1] * (hm[t, f, x + 2] - v)
                + wx[f, x] * (hm[t, f, x] - v)
                + (flux - pltpu.roll(flux, 1, 0))
                + wzp[f, x] * (up - v)
                + wzm[f, x] * (down - v)
            )
            olds.append(v)
            news.append(v + total)
        trade = ra[x] * olds[0] - rb[x] * olds[1]
        return news[0] - trade, news[1] + trade

    def sense_plane(t, slot, x):
        u = ck[slot, x + 1]
        v = hm[t, 0, x + 1]
        u_up, u_down = along_z(u, zchalo[slot], x)
        v_up, v_down = along_z(v, zhalo[t], x)
        across = (pltpu.roll(u, ny - 1, 0) - u) * (pltpu.roll(v, ny - 1, 0) - v)
        across = jnp.where(no_up, 0.0, across)
        return (
            (ck[slot, x + 2] - u) * (hm[t, 0, x + 2] - v)
            + (ck[slot, x] - u) * (hm[t, 0, x] - v)
            + (across + pltpu.roll(across, 1, 0))
            + (u_up - u) * (v_up - v)
            + (u_down - u) * (v_down - v)
        )

    for swap in x_first:
        swap.recv()
    z_step[0].recv()
    merge(zsend.at[0], zlo.at[0], zhi.at[0], zhalo.at[0])
    for f in range(2):
        fill_x((hm.at[0, f, 0], hm.at[0, f, 1]), (hm.at[0, f, nx + 1], hm.at[0, f, nx]))
        fill_x((cf.at[f, 0], cf.at[f, 1]), (cf.at[f, nx + 1], cf.at[f, nx]))

    def weights(x):
        for f in range(2):
            c = cf[f, x + 1]
            up, down = along_z(c, zhalo[0], (2 + f) * nx + x)
            wx[f, x + 1] = 0.5 * (c + cf[f, x + 2])
            wy[f, x] = jnp.where(no_up, 0.0, 0.5 * (c + pltpu.roll(c, ny - 1, 0)))
            wzp[f, x] = 0.5 * (c + up)
            wzm[f, x] = 0.5 * (c + down)

    for f in range(2):
        wx[f, 0] = 0.5 * (cf[f, 0] + cf[f, 1])
    over(0, nx, weights)

    for t in range(steps):
        slot = slots[t]
        if t > 0:
            x_step[t].recv()
            z_step[t].recv()
            fill(x_step[t])
            merge(zsend.at[t], zlo.at[t], zhi.at[t], zhalo.at[t])
        if t < steps - 1:
            def put(x, t=t):
                h, m = advance_plane(t, x)
                hm[t + 1, 0, x + 1] = h
                hm[t + 1, 1, x + 1] = m

            put(0)
            put(last)
            x_step[t + 1].start()
            over(1, last, put)
            pack([hm[t + 1, f, x + 1] for f in range(2) for x in range(nx)], zsend.at[t + 1])
            z_step[t + 1].start()
        if t == 0:
            x_check.recv()
            z_check.recv()
            for s in range(steps):
                merge(zcsend.at[s], zclo.at[s], zchi.at[s], zchalo.at[s])
            fill_x((ck.at[:, 0], ck.at[:, 1]), (ck.at[:, nx + 1], ck.at[:, nx]))
        if t < steps - 1:
            def sense(x, t=t, slot=slot):
                g = sense_plane(t, slot, x)
                grad[x] = g if t == 0 else grad[x] + g

            over(0, nx, sense)
        else:
            def coarsen(i, carry, t=t, slot=slot):
                total = jnp.zeros((ny, nz), jnp.float32)
                for j in range(2):
                    x = 2 * i + j
                    g = -0.5 * (grad[x] + sense_plane(t, slot, x))
                    total = total + jnp.where(lab[x] == 0, g, 0.0)
                for p in range(n_x):
                    csend[p, i] = total[p * rows : (p + 1) * rows]
                return carry

            lax.fori_loop(0, nx // 2, coarsen, 0)

    spread = []
    for d in range(1, n_x):
        peer = lax.rem(gx + d, n_x)
        copy = pltpu.make_async_remote_copy(
            src_ref=csend.at[peer], dst_ref=crecv.at[gx],
            send_sem=c_send_sem.at[d], recv_sem=c_recv_sem.at[d],
            device_id=(peer, gz), device_id_type=MESH)
        copy.start()
        spread.append(copy)
    crecv[gx] = csend[gx]

    def finish(x):
        h, m = advance_plane(steps - 1, x)
        hm_out[0, x] = h
        hm_out[1, x] = m

    over(0, nx, finish)
    outs = [
        pltpu.make_async_copy(hm_out.at[0], out_h, local_sem.at[5]),
        pltpu.make_async_copy(hm_out.at[1], out_m, local_sem.at[6]),
    ]
    for copy in outs:
        copy.start()

    for copy in spread:
        copy.wait_recv()
    length = n_x * (nx // 2)
    pair_row = lax.broadcasted_iota(jnp.int32, (nz, nz // 2), 0)
    pair_col = lax.broadcasted_iota(jnp.int32, (nz, nz // 2), 1)
    first = 2 * pair_col
    pairs = jnp.where((pair_row == first) | (pair_row == first + 1), 1.0, 0.0)
    columns = [
        (crecv[:, :, 2 * k, :] + crecv[:, :, 2 * k + 1, :]).reshape(length, nz) for k in range(rows // 2)
    ]
    exact = dict(precision=lax.Precision.HIGHEST, preferred_element_type=jnp.float32)
    solved = jnp.dot(minv[...], jnp.concatenate(columns, axis=1), **exact)
    halves = jnp.dot(
        jnp.concatenate([solved[:, k * nz : (k + 1) * nz] for k in range(rows // 2)], axis=0), pairs, **exact
    )
    for k in range(rows // 2):
        out_s[:, k, :] = halves[k * length : (k + 1) * length]

    for copy in spread:
        copy.wait_send()
    for swap in x_first + [x_check, z_check] + x_step[1:] + z_step:
        swap.sent()
    for copy in outs:
        copy.wait()


def on_device(n_x, n_z, heat, moist, cond, labels, rates, exchange, checks, slots):
    nx, ny, nz = heat.shape
    steps = checks.shape[0]
    half = nx // 2
    length = n_x * half
    rows = ny // n_x
    f32 = jnp.float32
    hbm = pl.BlockSpec(memory_space=pl.ANY)
    smem = pl.BlockSpec(memory_space=pltpu.SMEM)
    vmem = pl.BlockSpec(memory_space=pltpu.VMEM)
    n_swaps = 7 + 2 * steps
    scratch = [
        pltpu.VMEM((steps, 2, nx + 2, ny, nz), f32),
        pltpu.VMEM((2, nx + 2, ny, nz), f32),
        pltpu.VMEM((steps, nx + 2, ny, nz), f32),
        pltpu.VMEM((nx, ny, nz), jnp.int32),
        pltpu.VMEM((nx, ny, nz), f32),
        pltpu.VMEM((nx, ny, nz), f32),
        pltpu.VMEM((2, nx + 1, ny, nz), f32),
        pltpu.VMEM((2, nx, ny, nz), f32),
        pltpu.VMEM((2, nx, ny, nz), f32),
        pltpu.VMEM((2, nx, ny, nz), f32),
    ] + [pltpu.VMEM((steps, ny, nz), f32) for _ in range(8)] + [
        pltpu.VMEM((nx, ny, nz), f32),
        pltpu.VMEM((2, nx, ny, nz), f32),
        pltpu.VMEM((n_x, half, rows, nz), f32),
        pltpu.VMEM((n_x, half, rows, nz), f32),
        pltpu.SemaphoreType.DMA((7,)),
        pltpu.SemaphoreType.DMA((2 * n_swaps,)),
        pltpu.SemaphoreType.DMA((2 * n_swaps,)),
        pltpu.SemaphoreType.DMA((n_x,)),
        pltpu.SemaphoreType.DMA((n_x,)),
    ]
    return pl.pallas_call(
        functools.partial(kernel, n_x, n_z, steps),
        out_shape=(
            jax.ShapeDtypeStruct(heat.shape, f32),
            jax.ShapeDtypeStruct(heat.shape, f32),
            jax.ShapeDtypeStruct((length, rows // 2, nz // 2), f32),
        ),
        in_specs=[hbm, hbm, hbm, hbm, smem, smem, hbm, smem, vmem],
        out_specs=(hbm, hbm, vmem),
        scratch_shapes=scratch,
        compiler_params=pltpu.CompilerParams(
            collective_id=0, has_side_effects=True, vmem_limit_bytes=62 * 1024 * 1024
        ),
        name="adjoint_window",
    )(heat, moist, cond, labels, rates, exchange, checks, slots, jnp.asarray(smoother(length)))


def solution(mesh):
    grid = P("gx", None, "gz")
    in_specs = (grid, grid, grid, grid, P(), P(), P(None, "gx", None, "gz"), P())
    out_specs = (grid, grid, P(None, "gx", "gz"))
    return jax.shard_map(
        functools.partial(on_device, mesh.shape["gx"], mesh.shape["gz"]),
        mesh=mesh, in_specs=in_specs, out_specs=out_specs, check_vma=False,
    )
```

```python
import functools

import jax
import jax.numpy as jnp
import numpy as np
from jax import lax
from jax.experimental import pallas as pl
from jax.experimental.pallas import tpu as pltpu
from jax.sharding import PartitionSpec as P

PRIOR_WEIGHT = 200.0
MESH = pl.DeviceIdType.MESH
TOGETHER = 4


def smoother(length):
    d = np.zeros((length, length))
    for i in range(length - 1):
        d[i, i] += 1.0
        d[i + 1, i + 1] += 1.0
        d[i, i + 1] -= 1.0
        d[i + 1, i] -= 1.0
    return np.linalg.inv(np.eye(length) + PRIOR_WEIGHT * d).astype(np.float32)


class Swap:
    def __init__(self, here, count, target, sems, index, low_face, high_face, low_halo, high_halo):
        send_sem, recv_sem = sems
        self.here, self.count = here, count
        self.faces = (low_face, high_face)
        self.halos = (low_halo, high_halo)
        self.down = pltpu.make_async_remote_copy(
            src_ref=low_face, dst_ref=high_halo,
            send_sem=send_sem.at[2 * index], recv_sem=recv_sem.at[2 * index],
            device_id=target(lax.rem(here + count - 1, count)), device_id_type=MESH)
        self.up = pltpu.make_async_remote_copy(
            src_ref=high_face, dst_ref=low_halo,
            send_sem=send_sem.at[2 * index + 1], recv_sem=recv_sem.at[2 * index + 1],
            device_id=target(lax.rem(here + 1, count)), device_id_type=MESH)

    def start(self):
        pl.when(self.here > 0)(self.down.start)
        pl.when(self.here < self.count - 1)(self.up.start)

    def recv(self):
        pl.when(self.here < self.count - 1)(self.down.wait_recv)
        pl.when(self.here > 0)(self.up.wait_recv)

    def sent(self):
        pl.when(self.here > 0)(self.down.wait_send)
        pl.when(self.here < self.count - 1)(self.up.wait_send)


def kernel(
    n_x, n_z, steps,
    heat, moist, cond, labels, rate_t, exch_t, checks, slots, minv,
    out_h, out_m, out_s,
    hm, cf, ck, lab, ra, rb, wx, wy, wzp, wzm,
    zsend, zlo, zhi, zhalo, zcsend, zclo, zchi, zchalo,
    grad, hm_out, csend, crecv,
    local_sem, send_sem, recv_sem, c_send_sem, c_recv_sem,
):
    nx, ny, nz = lab.shape
    rows = ny // n_x
    gx, gz = lax.axis_index("gx"), lax.axis_index("gz")
    sems = (send_sem, recv_sem)

    def over(low, high, body):
        def block(i, carry):
            for j in range(TOGETHER):
                body(low + i * TOGETHER + j)
            return carry

        lax.fori_loop(0, (high - low) // TOGETHER, block, 0)
        for x in range(low + (high - low) // TOGETHER * TOGETHER, high):
            body(x)

    to_x = lambda i: (i, gz)
    to_z = lambda i: (gx, i)
    inner = pl.ds(1, nx)

    locals_ = [
        pltpu.make_async_copy(labels, lab, local_sem.at[0]),
        pltpu.make_async_copy(heat, hm.at[0, 0, inner], local_sem.at[1]),
        pltpu.make_async_copy(moist, hm.at[0, 1, inner], local_sem.at[2]),
        pltpu.make_async_copy(cond, cf.at[0, inner], local_sem.at[3]),
        pltpu.make_async_copy(checks, ck.at[:, inner], local_sem.at[4]),
    ]
    for copy in locals_:
        copy.start()

    barrier = pltpu.get_barrier_semaphore()
    for d in range(1, n_x):
        pl.semaphore_signal(barrier, inc=1, device_id=(lax.rem(gx + d, n_x), gz), device_id_type=MESH)

    @pl.when(gz > 0)
    def _():
        pl.semaphore_signal(barrier, inc=1, device_id=(gx, gz - 1), device_id_type=MESH)

    @pl.when(gz < n_z - 1)
    def _():
        pl.semaphore_signal(barrier, inc=1, device_id=(gx, gz + 1), device_id_type=MESH)

    def x_swap(index, low_face, high_face, low_halo, high_halo):
        return Swap(gx, n_x, to_x, sems, index, low_face, high_face, low_halo, high_halo)

    def z_swap(index, low_face, high_face, low_halo, high_halo):
        return Swap(gz, n_z, to_z, sems, index, low_face, high_face, low_halo, high_halo)

    last = nx - 1
    x_first = [
        x_swap(0, heat.at[0], heat.at[last], hm.at[0, 0, 0], hm.at[0, 0, nx + 1]),
        x_swap(1, moist.at[0], moist.at[last], hm.at[0, 1, 0], hm.at[0, 1, nx + 1]),
        x_swap(2, cond.at[0], cond.at[last], cf.at[0, 0], cf.at[0, nx + 1]),
        x_swap(3, cf.at[1, 1], cf.at[1, nx], cf.at[1, 0], cf.at[1, nx + 1]),
    ]
    x_check = x_swap(4, checks.at[:, 0], checks.at[:, last], ck.at[:, 0], ck.at[:, nx + 1])
    z_check = z_swap(5, zcsend, zcsend, zclo, zchi)
    x_step = [None] + [
        x_swap(5 + t, hm.at[t, :, 1], hm.at[t, :, nx], hm.at[t, :, 0], hm.at[t, :, nx + 1])
        for t in range(1, steps)
    ]
    z_step = [
        z_swap(5 + steps + t, zsend.at[t], zsend.at[t], zlo.at[t], zhi.at[t])
        for t in range(steps)
    ]

    lane = lax.broadcasted_iota(jnp.int32, (ny, nz), 1)
    row = lax.broadcasted_iota(jnp.int32, (ny, nz), 0)
    at_first, at_last = lane == 0, lane == nz - 1
    no_up = row == ny - 1
    pair = lax.shift_right_logical(lane, 1)
    even = lax.rem(lane, 2) == 0

    def pick(label, table):
        return jnp.where(label == 0, table[0], jnp.where(label == 1, table[1], jnp.where(label == 2, table[2], table[3])))

    locals_[0].wait()
    table_m = [rate_t[i] for i in range(4)]
    table_a = [exch_t[0, i] for i in range(4)]
    table_b = [exch_t[1, i] for i in range(4)]

    def rates(x):
        label = lab[x]
        cf[1, x + 1] = pick(label, table_m)
        ra[x] = pick(label, table_a)
        rb[x] = pick(label, table_b)

    over(0, nx, rates)

    def pack(planes, ref):
        total = jnp.zeros((ny, nz), jnp.float32)
        for j, v in enumerate(planes):
            total = jnp.where(pair == j, pltpu.roll(v, (2 * j + 1) % nz, 1), total)
        ref[...] = total

    def merge(own, low_pack, high_pack, ref):
        ref[...] = own[...]

        @pl.when(gz > 0)
        def _():
            ref[...] = jnp.where(even, ref[...], pltpu.roll(low_pack[...], 1, 1))

        @pl.when(gz < n_z - 1)
        def _():
            ref[...] = jnp.where(even, pltpu.roll(high_pack[...], nz - 1, 1), ref[...])

    for copy in locals_[1:4]:
        copy.wait()
    pack([src[i, x + 1] for src in (hm.at[0], cf) for i in range(2) for x in range(nx)], zsend.at[0])
    beside = jnp.where(gz > 0, 1, 0) + jnp.where(gz < n_z - 1, 1, 0)
    pl.semaphore_wait(barrier, n_x - 1 + beside)
    z_step[0].start()
    for swap in x_first:
        swap.start()
    x_check.start()
    locals_[4].wait()
    for s in range(steps):
        pack([ck[s, x + 1] for x in range(nx)], zcsend.at[s])
    z_check.start()

    def fill(swap):
        @pl.when(swap.here == 0)
        def _():
            swap.halos[0][...] = swap.faces[0][...]

        @pl.when(swap.here == swap.count - 1)
        def _():
            swap.halos[1][...] = swap.faces[1][...]

    def fill_x(here_lo, here_hi):
        @pl.when(gx == 0)
        def _():
            here_lo[0][...] = here_lo[1][...]

        @pl.when(gx == n_x - 1)
        def _():
            here_hi[0][...] = here_hi[1][...]

    def along_z(v, halo, j):
        ends = pltpu.roll(halo, nz - 1 - 2 * j, 1)
        up = jnp.where(at_last, ends, pltpu.roll(v, nz - 1, 1))
        down = jnp.where(at_first, ends, pltpu.roll(v, 1, 1))
        return up, down

    def advance_plane(t, x):
        news = []
        olds = []
        for f in range(2):
            v = hm[t, f, x + 1]
            up, down = along_z(v, zhalo[t], f * nx + x)
            flux = wy[f, x] * (pltpu.roll(v, ny - 1, 0) - v)
            total = (
                wx[f, x + 1] * (hm[t, f, x + 2] - v)
                + wx[f, x] * (hm[t, f, x] - v)
                + (flux - pltpu.roll(flux, 1, 0))
                + wzp[f, x] * (up - v)
                + wzm[f, x] * (down - v)
            )
            olds.append(v)
            news.append(v + total)
        trade = ra[x] * olds[0] - rb[x] * olds[1]
        return news[0] - trade, news[1] + trade

    def sense_plane(t, slot, x):
        u = ck[slot, x + 1]
        v = hm[t, 0, x + 1]
        u_up, u_down = along_z(u, zchalo[slot], x)
        v_up, v_down = along_z(v, zhalo[t], x)
        across = (pltpu.roll(u, ny - 1, 0) - u) * (pltpu.roll(v, ny - 1, 0) - v)
        across = jnp.where(no_up, 0.0, across)
        return (
            (ck[slot, x + 2] - u) * (hm[t, 0, x + 2] - v)
            + (ck[slot, x] - u) * (hm[t, 0, x] - v)
            + (across + pltpu.roll(across, 1, 0))
            + (u_up - u) * (v_up - v)
            + (u_down - u) * (v_down - v)
        )

    for swap in x_first:
        swap.recv()
    z_step[0].recv()
    merge(zsend.at[0], zlo.at[0], zhi.at[0], zhalo.at[0])
    for f in range(2):
        fill_x((hm.at[0, f, 0], hm.at[0, f, 1]), (hm.at[0, f, nx + 1], hm.at[0, f, nx]))
        fill_x((cf.at[f, 0], cf.at[f, 1]), (cf.at[f, nx + 1], cf.at[f, nx]))

    def weights(x):
        for f in range(2):
            c = cf[f, x + 1]
            up, down = along_z(c, zhalo[0], (2 + f) * nx + x)
            wx[f, x + 1] = 0.5 * (c + cf[f, x + 2])
            wy[f, x] = jnp.where(no_up, 0.0, 0.5 * (c + pltpu.roll(c, ny - 1, 0)))
            wzp[f, x] = 0.5 * (c + up)
            wzm[f, x] = 0.5 * (c + down)

    for f in range(2):
        wx[f, 0] = 0.5 * (cf[f, 0] + cf[f, 1])
    over(0, nx, weights)

    for t in range(steps):
        slot = slots[t]
        if t > 0:
            x_step[t].recv()
            z_step[t].recv()
            fill(x_step[t])
            merge(zsend.at[t], zlo.at[t], zhi.at[t], zhalo.at[t])
        if t < steps - 1:
            def put(x, t=t):
                h, m = advance_plane(t, x)
                hm[t + 1, 0, x + 1] = h
                hm[t + 1, 1, x + 1] = m

            put(0)
            put(last)
            x_step[t + 1].start()
            over(1, last, put)
            pack([hm[t + 1, f, x + 1] for f in range(2) for x in range(nx)], zsend.at[t + 1])
            z_step[t + 1].start()
        if t == 0:
            x_check.recv()
            z_check.recv()
            for s in range(steps):
                merge(zcsend.at[s], zclo.at[s], zchi.at[s], zchalo.at[s])
            fill_x((ck.at[:, 0], ck.at[:, 1]), (ck.at[:, nx + 1], ck.at[:, nx]))
        if t < steps - 1:
            def sense(x, t=t, slot=slot):
                g = sense_plane(t, slot, x)
                grad[x] = g if t == 0 else grad[x] + g

            over(0, nx, sense)
        else:
            def coarsen(i, carry, t=t, slot=slot):
                total = jnp.zeros((ny, nz), jnp.float32)
                for j in range(2):
                    x = 2 * i + j
                    g = -0.5 * (grad[x] + sense_plane(t, slot, x))
                    total = total + jnp.where(lab[x] == 0, g, 0.0)
                for p in range(n_x):
                    csend[p, i] = total[p * rows : (p + 1) * rows]
                return carry

            lax.fori_loop(0, nx // 2, coarsen, 0)

    spread = []
    for d in range(1, n_x):
        peer = lax.rem(gx + d, n_x)
        copy = pltpu.make_async_remote_copy(
            src_ref=csend.at[peer], dst_ref=crecv.at[gx],
            send_sem=c_send_sem.at[d], recv_sem=c_recv_sem.at[d],
            device_id=(peer, gz), device_id_type=MESH)
        copy.start()
        spread.append(copy)
    crecv[gx] = csend[gx]

    def finish(x):
        h, m = advance_plane(steps - 1, x)
        hm_out[0, x] = h
        hm_out[1, x] = m

    over(0, nx, finish)
    outs = [
        pltpu.make_async_copy(hm_out.at[0], out_h, local_sem.at[5]),
        pltpu.make_async_copy(hm_out.at[1], out_m, local_sem.at[6]),
    ]
    for copy in outs:
        copy.start()

    for copy in spread:
        copy.wait_recv()
    length = n_x * (nx // 2)
    pair_row = lax.broadcasted_iota(jnp.int32, (nz, nz // 2), 0)
    pair_col = lax.broadcasted_iota(jnp.int32, (nz, nz // 2), 1)
    first = 2 * pair_col
    pairs = jnp.where((pair_row == first) | (pair_row == first + 1), 1.0, 0.0)
    columns = [
        (crecv[:, :, 2 * k, :] + crecv[:, :, 2 * k + 1, :]).reshape(length, nz) for k in range(rows // 2)
    ]
    exact = dict(precision=lax.Precision.HIGHEST, preferred_element_type=jnp.float32)
    solved = jnp.dot(minv[...], jnp.concatenate(columns, axis=1), **exact)
    halves = jnp.dot(
        jnp.concatenate([solved[:, k * nz : (k + 1) * nz] for k in range(rows // 2)], axis=0), pairs, **exact
    )
    for k in range(rows // 2):
        out_s[:, k, :] = halves[k * length : (k + 1) * length]

    for copy in spread:
        copy.wait_send()
    for swap in x_first + [x_check, z_check] + x_step[1:] + z_step:
        swap.sent()
    for copy in outs:
        copy.wait()


def hand_on(*refs):
    for i in range(3):
        refs[3 + i][...] = refs[i][...]


def on_device(n_x, n_z, heat, moist, cond, labels, rates, exchange, checks, slots):
    nx, ny, nz = heat.shape
    steps = checks.shape[0]
    half = nx // 2
    length = n_x * half
    rows = ny // n_x
    f32 = jnp.float32
    hbm = pl.BlockSpec(memory_space=pl.ANY)
    smem = pl.BlockSpec(memory_space=pltpu.SMEM)
    vmem = pl.BlockSpec(memory_space=pltpu.VMEM)
    n_swaps = 7 + 2 * steps
    scratch = [
        pltpu.VMEM((steps, 2, nx + 2, ny, nz), f32),
        pltpu.VMEM((2, nx + 2, ny, nz), f32),
        pltpu.VMEM((steps, nx + 2, ny, nz), f32),
        pltpu.VMEM((nx, ny, nz), jnp.int32),
        pltpu.VMEM((nx, ny, nz), f32),
        pltpu.VMEM((nx, ny, nz), f32),
        pltpu.VMEM((2, nx + 1, ny, nz), f32),
        pltpu.VMEM((2, nx, ny, nz), f32),
        pltpu.VMEM((2, nx, ny, nz), f32),
        pltpu.VMEM((2, nx, ny, nz), f32),
    ] + [pltpu.VMEM((steps, ny, nz), f32) for _ in range(8)] + [
        pltpu.VMEM((nx, ny, nz), f32),
        pltpu.VMEM((2, nx, ny, nz), f32),
        pltpu.VMEM((n_x, half, rows, nz), f32),
        pltpu.VMEM((n_x, half, rows, nz), f32),
        pltpu.SemaphoreType.DMA((7,)),
        pltpu.SemaphoreType.DMA((2 * n_swaps,)),
        pltpu.SemaphoreType.DMA((2 * n_swaps,)),
        pltpu.SemaphoreType.DMA((n_x,)),
        pltpu.SemaphoreType.DMA((n_x,)),
    ]
    done = pl.pallas_call(
        functools.partial(kernel, n_x, n_z, steps),
        out_shape=(
            jax.ShapeDtypeStruct(heat.shape, f32),
            jax.ShapeDtypeStruct(heat.shape, f32),
            jax.ShapeDtypeStruct((length, rows // 2, nz // 2), f32),
        ),
        in_specs=[hbm, hbm, hbm, hbm, smem, smem, hbm, smem, vmem],
        out_specs=(hbm, hbm, vmem),
        scratch_shapes=scratch,
        compiler_params=pltpu.CompilerParams(
            collective_id=0, has_side_effects=True, vmem_limit_bytes=62 * 1024 * 1024
        ),
        name="adjoint_window",
    )(heat, moist, cond, labels, rates, exchange, checks, slots, jnp.asarray(smoother(length)))
    return pl.pallas_call(
        hand_on,
        out_shape=tuple(jax.ShapeDtypeStruct(a.shape, a.dtype) for a in done),
        in_specs=[vmem] * 3,
        out_specs=(vmem,) * 3,
        compiler_params=pltpu.CompilerParams(vmem_limit_bytes=62 * 1024 * 1024),
        name="hand_on",
    )(*done)


def solution(mesh):
    grid = P("gx", None, "gz")
    in_specs = (grid, grid, grid, grid, P(), P(), P(None, "gx", None, "gz"), P())
    out_specs = (grid, grid, P(None, "gx", "gz"))
    return jax.shard_map(
        functools.partial(on_device, mesh.shape["gx"], mesh.shape["gz"]),
        mesh=mesh, in_specs=in_specs, out_specs=out_specs, check_vma=False,
    )
```

```python
import functools

import jax
import jax.numpy as jnp
import numpy as np
from jax import lax
from jax.experimental import pallas as pl
from jax.experimental.pallas import tpu as pltpu
from jax.sharding import PartitionSpec as P

PRIOR_WEIGHT = 200.0
MESH = pl.DeviceIdType.MESH
TOGETHER = 8


def smoother(length):
    d = np.zeros((length, length))
    for i in range(length - 1):
        d[i, i] += 1.0
        d[i + 1, i + 1] += 1.0
        d[i, i + 1] -= 1.0
        d[i + 1, i] -= 1.0
    return np.linalg.inv(np.eye(length) + PRIOR_WEIGHT * d).astype(np.float32)


class Swap:
    def __init__(self, here, count, target, sems, index, low_face, high_face, low_halo, high_halo):
        send_sem, recv_sem = sems
        self.here, self.count = here, count
        self.faces = (low_face, high_face)
        self.halos = (low_halo, high_halo)
        self.down = pltpu.make_async_remote_copy(
            src_ref=low_face, dst_ref=high_halo,
            send_sem=send_sem.at[2 * index], recv_sem=recv_sem.at[2 * index],
            device_id=target(lax.rem(here + count - 1, count)), device_id_type=MESH)
        self.up = pltpu.make_async_remote_copy(
            src_ref=high_face, dst_ref=low_halo,
            send_sem=send_sem.at[2 * index + 1], recv_sem=recv_sem.at[2 * index + 1],
            device_id=target(lax.rem(here + 1, count)), device_id_type=MESH)

    def start(self):
        pl.when(self.here > 0)(self.down.start)
        pl.when(self.here < self.count - 1)(self.up.start)

    def recv(self):
        pl.when(self.here < self.count - 1)(self.down.wait_recv)
        pl.when(self.here > 0)(self.up.wait_recv)

    def sent(self):
        pl.when(self.here > 0)(self.down.wait_send)
        pl.when(self.here < self.count - 1)(self.up.wait_send)


def kernel(
    n_x, n_z, steps,
    heat, moist, cond, labels, rate_t, exch_t, checks, slots, minv,
    out_h, out_m, out_s,
    hm, cf, ck, lab, ra, rb, wx, wy, wzp, wzm,
    zsend, zlo, zhi, zhalo, zcsend, zclo, zchi, zchalo,
    grad, hm_out, csend, crecv,
    local_sem, send_sem, recv_sem, c_send_sem, c_recv_sem,
):
    nx, ny, nz = lab.shape
    rows = ny // n_x
    gx, gz = lax.axis_index("gx"), lax.axis_index("gz")
    sems = (send_sem, recv_sem)

    def over(low, high, body):
        def block(i, carry):
            for j in range(TOGETHER):
                body(low + i * TOGETHER + j)
            return carry

        lax.fori_loop(0, (high - low) // TOGETHER, block, 0)
        for x in range(low + (high - low) // TOGETHER * TOGETHER, high):
            body(x)

    to_x = lambda i: (i, gz)
    to_z = lambda i: (gx, i)
    inner = pl.ds(1, nx)

    locals_ = [
        pltpu.make_async_copy(labels, lab, local_sem.at[0]),
        pltpu.make_async_copy(heat, hm.at[0, 0, inner], local_sem.at[1]),
        pltpu.make_async_copy(moist, hm.at[0, 1, inner], local_sem.at[2]),
        pltpu.make_async_copy(cond, cf.at[0, inner], local_sem.at[3]),
        pltpu.make_async_copy(checks, ck.at[:, inner], local_sem.at[4]),
    ]
    for copy in locals_:
        copy.start()

    barrier = pltpu.get_barrier_semaphore()
    for d in range(1, n_x):
        pl.semaphore_signal(barrier, inc=1, device_id=(lax.rem(gx + d, n_x), gz), device_id_type=MESH)

    @pl.when(gz > 0)
    def _():
        pl.semaphore_signal(barrier, inc=1, device_id=(gx, gz - 1), device_id_type=MESH)

    @pl.when(gz < n_z - 1)
    def _():
        pl.semaphore_signal(barrier, inc=1, device_id=(gx, gz + 1), device_id_type=MESH)

    def x_swap(index, low_face, high_face, low_halo, high_halo):
        return Swap(gx, n_x, to_x, sems, index, low_face, high_face, low_halo, high_halo)

    def z_swap(index, low_face, high_face, low_halo, high_halo):
        return Swap(gz, n_z, to_z, sems, index, low_face, high_face, low_halo, high_halo)

    last = nx - 1
    x_first = [
        x_swap(0, heat.at[0], heat.at[last], hm.at[0, 0, 0], hm.at[0, 0, nx + 1]),
        x_swap(1, moist.at[0], moist.at[last], hm.at[0, 1, 0], hm.at[0, 1, nx + 1]),
        x_swap(2, cond.at[0], cond.at[last], cf.at[0, 0], cf.at[0, nx + 1]),
        x_swap(3, cf.at[1, 1], cf.at[1, nx], cf.at[1, 0], cf.at[1, nx + 1]),
    ]
    x_check = x_swap(4, checks.at[:, 0], checks.at[:, last], ck.at[:, 0], ck.at[:, nx + 1])
    z_check = z_swap(5, zcsend, zcsend, zclo, zchi)
    x_step = [None] + [
        x_swap(5 + t, hm.at[t, :, 1], hm.at[t, :, nx], hm.at[t, :, 0], hm.at[t, :, nx + 1])
        for t in range(1, steps)
    ]
    z_step = [
        z_swap(5 + steps + t, zsend.at[t], zsend.at[t], zlo.at[t], zhi.at[t])
        for t in range(steps)
    ]

    lane = lax.broadcasted_iota(jnp.int32, (ny, nz), 1)
    row = lax.broadcasted_iota(jnp.int32, (ny, nz), 0)
    at_first, at_last = lane == 0, lane == nz - 1
    no_up = row == ny - 1
    pair = lax.shift_right_logical(lane, 1)
    even = lax.rem(lane, 2) == 0

    def pick(label, table):
        return jnp.where(label == 0, table[0], jnp.where(label == 1, table[1], jnp.where(label == 2, table[2], table[3])))

    locals_[0].wait()
    table_m = [rate_t[i] for i in range(4)]
    table_a = [exch_t[0, i] for i in range(4)]
    table_b = [exch_t[1, i] for i in range(4)]

    def rates(x):
        label = lab[x]
        cf[1, x + 1] = pick(label, table_m)
        ra[x] = pick(label, table_a)
        rb[x] = pick(label, table_b)

    over(0, nx, rates)

    def pack(planes, ref):
        total = jnp.zeros((ny, nz), jnp.float32)
        for j, v in enumerate(planes):
            total = jnp.where(pair == j, pltpu.roll(v, (2 * j + 1) % nz, 1), total)
        ref[...] = total

    def merge(own, low_pack, high_pack, ref):
        ref[...] = own[...]

        @pl.when(gz > 0)
        def _():
            ref[...] = jnp.where(even, ref[...], pltpu.roll(low_pack[...], 1, 1))

        @pl.when(gz < n_z - 1)
        def _():
            ref[...] = jnp.where(even, pltpu.roll(high_pack[...], nz - 1, 1), ref[...])

    for copy in locals_[1:4]:
        copy.wait()
    pack([src[i, x + 1] for src in (hm.at[0], cf) for i in range(2) for x in range(nx)], zsend.at[0])
    beside = jnp.where(gz > 0, 1, 0) + jnp.where(gz < n_z - 1, 1, 0)
    pl.semaphore_wait(barrier, n_x - 1 + beside)
    z_step[0].start()
    for swap in x_first:
        swap.start()
    x_check.start()
    locals_[4].wait()
    for s in range(steps):
        pack([ck[s, x + 1] for x in range(nx)], zcsend.at[s])
    z_check.start()

    def fill(swap):
        @pl.when(swap.here == 0)
        def _():
            swap.halos[0][...] = swap.faces[0][...]

        @pl.when(swap.here == swap.count - 1)
        def _():
            swap.halos[1][...] = swap.faces[1][...]

    def fill_x(here_lo, here_hi):
        @pl.when(gx == 0)
        def _():
            here_lo[0][...] = here_lo[1][...]

        @pl.when(gx == n_x - 1)
        def _():
            here_hi[0][...] = here_hi[1][...]

    def along_z(v, halo, j):
        ends = pltpu.roll(halo, nz - 1 - 2 * j, 1)
        up = jnp.where(at_last, ends, pltpu.roll(v, nz - 1, 1))
        down = jnp.where(at_first, ends, pltpu.roll(v, 1, 1))
        return up, down

    def advance_plane(t, x):
        news = []
        olds = []
        for f in range(2):
            v = hm[t, f, x + 1]
            up, down = along_z(v, zhalo[t], f * nx + x)
            flux = wy[f, x] * (pltpu.roll(v, ny - 1, 0) - v)
            total = (
                wx[f, x + 1] * (hm[t, f, x + 2] - v)
                + wx[f, x] * (hm[t, f, x] - v)
                + (flux - pltpu.roll(flux, 1, 0))
                + wzp[f, x] * (up - v)
                + wzm[f, x] * (down - v)
            )
            olds.append(v)
            news.append(v + total)
        trade = ra[x] * olds[0] - rb[x] * olds[1]
        return news[0] - trade, news[1] + trade

    def sense_plane(t, slot, x):
        u = ck[slot, x + 1]
        v = hm[t, 0, x + 1]
        u_up, u_down = along_z(u, zchalo[slot], x)
        v_up, v_down = along_z(v, zhalo[t], x)
        across = (pltpu.roll(u, ny - 1, 0) - u) * (pltpu.roll(v, ny - 1, 0) - v)
        across = jnp.where(no_up, 0.0, across)
        return (
            (ck[slot, x + 2] - u) * (hm[t, 0, x + 2] - v)
            + (ck[slot, x] - u) * (hm[t, 0, x] - v)
            + (across + pltpu.roll(across, 1, 0))
            + (u_up - u) * (v_up - v)
            + (u_down - u) * (v_down - v)
        )

    for swap in x_first:
        swap.recv()
    z_step[0].recv()
    merge(zsend.at[0], zlo.at[0], zhi.at[0], zhalo.at[0])
    for f in range(2):
        fill_x((hm.at[0, f, 0], hm.at[0, f, 1]), (hm.at[0, f, nx + 1], hm.at[0, f, nx]))
        fill_x((cf.at[f, 0], cf.at[f, 1]), (cf.at[f, nx + 1], cf.at[f, nx]))

    def weights(x):
        for f in range(2):
            c = cf[f, x + 1]
            up, down = along_z(c, zhalo[0], (2 + f) * nx + x)
            wx[f, x + 1] = 0.5 * (c + cf[f, x + 2])
            wy[f, x] = jnp.where(no_up, 0.0, 0.5 * (c + pltpu.roll(c, ny - 1, 0)))
            wzp[f, x] = 0.5 * (c + up)
            wzm[f, x] = 0.5 * (c + down)

    for f in range(2):
        wx[f, 0] = 0.5 * (cf[f, 0] + cf[f, 1])
    over(0, nx, weights)

    for t in range(steps):
        slot = slots[t]
        if t > 0:
            x_step[t].recv()
            z_step[t].recv()
            fill(x_step[t])
            merge(zsend.at[t], zlo.at[t], zhi.at[t], zhalo.at[t])
        if t < steps - 1:
            def put(x, t=t):
                h, m = advance_plane(t, x)
                hm[t + 1, 0, x + 1] = h
                hm[t + 1, 1, x + 1] = m

            put(0)
            put(last)
            x_step[t + 1].start()
            over(1, last, put)
            pack([hm[t + 1, f, x + 1] for f in range(2) for x in range(nx)], zsend.at[t + 1])
            z_step[t + 1].start()
        if t == 0:
            x_check.recv()
            z_check.recv()
            for s in range(steps):
                merge(zcsend.at[s], zclo.at[s], zchi.at[s], zchalo.at[s])
            fill_x((ck.at[:, 0], ck.at[:, 1]), (ck.at[:, nx + 1], ck.at[:, nx]))
        if t < steps - 1:
            def sense(x, t=t, slot=slot):
                g = sense_plane(t, slot, x)
                grad[x] = g if t == 0 else grad[x] + g

            over(0, nx, sense)
        else:
            def coarsen(i, carry, t=t, slot=slot):
                total = jnp.zeros((ny, nz), jnp.float32)
                for j in range(2):
                    x = 2 * i + j
                    g = -0.5 * (grad[x] + sense_plane(t, slot, x))
                    total = total + jnp.where(lab[x] == 0, g, 0.0)
                for p in range(n_x):
                    csend[p, i] = total[p * rows : (p + 1) * rows]
                return carry

            lax.fori_loop(0, nx // 2, coarsen, 0)

    spread = []
    for d in range(1, n_x):
        peer = lax.rem(gx + d, n_x)
        copy = pltpu.make_async_remote_copy(
            src_ref=csend.at[peer], dst_ref=crecv.at[gx],
            send_sem=c_send_sem.at[d], recv_sem=c_recv_sem.at[d],
            device_id=(peer, gz), device_id_type=MESH)
        copy.start()
        spread.append(copy)
    crecv[gx] = csend[gx]

    def finish(x):
        h, m = advance_plane(steps - 1, x)
        hm_out[0, x] = h
        hm_out[1, x] = m

    over(0, nx, finish)
    outs = [
        pltpu.make_async_copy(hm_out.at[0], out_h, local_sem.at[5]),
        pltpu.make_async_copy(hm_out.at[1], out_m, local_sem.at[6]),
    ]
    for copy in outs:
        copy.start()

    for copy in spread:
        copy.wait_recv()
    length = n_x * (nx // 2)
    pair_row = lax.broadcasted_iota(jnp.int32, (nz, nz // 2), 0)
    pair_col = lax.broadcasted_iota(jnp.int32, (nz, nz // 2), 1)
    first = 2 * pair_col
    pairs = jnp.where((pair_row == first) | (pair_row == first + 1), 1.0, 0.0)
    columns = [
        (crecv[:, :, 2 * k, :] + crecv[:, :, 2 * k + 1, :]).reshape(length, nz) for k in range(rows // 2)
    ]
    exact = dict(precision=lax.Precision.HIGHEST, preferred_element_type=jnp.float32)
    solved = jnp.dot(minv[...], jnp.concatenate(columns, axis=1), **exact)
    halves = jnp.dot(
        jnp.concatenate([solved[:, k * nz : (k + 1) * nz] for k in range(rows // 2)], axis=0), pairs, **exact
    )
    for k in range(rows // 2):
        out_s[:, k, :] = halves[k * length : (k + 1) * length]

    for copy in spread:
        copy.wait_send()
    for swap in x_first + [x_check, z_check] + x_step[1:] + z_step:
        swap.sent()
    for copy in outs:
        copy.wait()


def hand_on(*refs):
    for i in range(3):
        refs[3 + i][...] = refs[i][...]


def on_device(n_x, n_z, heat, moist, cond, labels, rates, exchange, checks, slots):
    nx, ny, nz = heat.shape
    steps = checks.shape[0]
    half = nx // 2
    length = n_x * half
    rows = ny // n_x
    f32 = jnp.float32
    hbm = pl.BlockSpec(memory_space=pl.ANY)
    smem = pl.BlockSpec(memory_space=pltpu.SMEM)
    vmem = pl.BlockSpec(memory_space=pltpu.VMEM)
    n_swaps = 7 + 2 * steps
    scratch = [
        pltpu.VMEM((steps, 2, nx + 2, ny, nz), f32),
        pltpu.VMEM((2, nx + 2, ny, nz), f32),
        pltpu.VMEM((steps, nx + 2, ny, nz), f32),
        pltpu.VMEM((nx, ny, nz), jnp.int32),
        pltpu.VMEM((nx, ny, nz), f32),
        pltpu.VMEM((nx, ny, nz), f32),
        pltpu.VMEM((2, nx + 1, ny, nz), f32),
        pltpu.VMEM((2, nx, ny, nz), f32),
        pltpu.VMEM((2, nx, ny, nz), f32),
        pltpu.VMEM((2, nx, ny, nz), f32),
    ] + [pltpu.VMEM((steps, ny, nz), f32) for _ in range(8)] + [
        pltpu.VMEM((nx, ny, nz), f32),
        pltpu.VMEM((2, nx, ny, nz), f32),
        pltpu.VMEM((n_x, half, rows, nz), f32),
        pltpu.VMEM((n_x, half, rows, nz), f32),
        pltpu.SemaphoreType.DMA((7,)),
        pltpu.SemaphoreType.DMA((2 * n_swaps,)),
        pltpu.SemaphoreType.DMA((2 * n_swaps,)),
        pltpu.SemaphoreType.DMA((n_x,)),
        pltpu.SemaphoreType.DMA((n_x,)),
    ]
    done = pl.pallas_call(
        functools.partial(kernel, n_x, n_z, steps),
        out_shape=(
            jax.ShapeDtypeStruct(heat.shape, f32),
            jax.ShapeDtypeStruct(heat.shape, f32),
            jax.ShapeDtypeStruct((length, rows // 2, nz // 2), f32),
        ),
        in_specs=[hbm, hbm, hbm, hbm, smem, smem, hbm, smem, vmem],
        out_specs=(hbm, hbm, vmem),
        scratch_shapes=scratch,
        compiler_params=pltpu.CompilerParams(
            collective_id=0, has_side_effects=True, vmem_limit_bytes=62 * 1024 * 1024
        ),
        name="adjoint_window",
    )(heat, moist, cond, labels, rates, exchange, checks, slots, jnp.asarray(smoother(length)))
    return pl.pallas_call(
        hand_on,
        out_shape=tuple(jax.ShapeDtypeStruct(a.shape, a.dtype) for a in done),
        in_specs=[vmem] * 3,
        out_specs=(vmem,) * 3,
        compiler_params=pltpu.CompilerParams(vmem_limit_bytes=62 * 1024 * 1024),
        name="hand_on",
    )(*done)


def solution(mesh):
    grid = P("gx", None, "gz")
    in_specs = (grid, grid, grid, grid, P(), P(), P(None, "gx", None, "gz"), P())
    out_specs = (grid, grid, P(None, "gx", "gz"))
    return jax.shard_map(
        functools.partial(on_device, mesh.shape["gx"], mesh.shape["gz"]),
        mesh=mesh, in_specs=in_specs, out_specs=out_specs, check_vma=False,
    )
```
